32 devices in a mesh: expert: 4 (over y, x), tp: 8 (over z, core).
Axes of the slice: x: 2, y: 2, z: 4, core: 2. Of those that a mesh axis runs over, the one named last changes fastest.
Arguments:
- tokens_in: bfloat16 [512, 3072], P(('expert', 'tp')), may hold values from -6 to 6
- grad_out: bfloat16 [512, 3072], P(('expert', 'tp')), may hold values from -6 to 6
- expert_ids: int32 [512, 2], P(('expert', 'tp')), may hold values from 0 to 3, all different within a row; in each aligned block of 16 rows (0 to 15, 16 to 31, ...) at most 8 rows name the same one
- combine: float32 [512, 2], P(('expert', 'tp')), may hold values from 0.2 to 1
- w_gate: bfloat16 [4, 3072, 8192], P('expert', None, 'tp'), may hold values from -0.109375 to 0.109375
- w_up: bfloat16 [4, 3072, 8192], P('expert', None, 'tp'), may hold values from -0.109375 to 0.109375
- w_down: bfloat16 [4, 8192, 3072], P('expert', 'tp'), may hold values from -0.0625 to 0.0625
Outputs:
- grad_input: bfloat16 [512, 3072], P(('expert', 'tp'))
- grad_gate: bfloat16 [4, 3072, 8192], P('expert', None, 'tp')
- grad_up: bfloat16 [4, 3072, 8192], P('expert', None, 'tp')
- grad_down: bfloat16 [4, 8192, 3072], P('expert', 'tp')
The draws below stay inside these ranges and needn't reach their ends.
Inputs may be any that keep to these rules, and one draw needn't show every extreme that they name: `expert_ids`: the two ids of a row differ. In each aligned block of 16 rows (the tokens of one device) no expert is named by more than 8 rows, and some block names some expert exactly 8 times.
All inputs are finite; a program needn't handle non-finite values.
Results may differ from the reference program's by a relative error of at most 0.0065.
Values may be sent and summed in bfloat16 or wider, within the bound.
A program may use at most 128 MiB of HBM per device.

```python
import math
import jax
import jax.numpy as jnp
import numpy as np
from jax import lax

D = 3072
FF = 8192
TOK_DEV = 16
CAP = 8
EXPERTS = 4
TOKENS = 512


def steps_of(key, extent, cuts, least, largest):
    gain = 1.0
    for dim, shards_of in cuts:
        steps = jax.random.uniform(jax.random.fold_in(jax.random.fold_in(key, 6), dim), (shards_of,), jnp.float32, least / len(cuts), largest / len(cuts))
        gain = gain * jnp.repeat(jnp.exp(steps), extent[dim] // shards_of).reshape((-1,) + (1,) * (len(extent) - 1 - dim))
    return gain


def deal_out(own_key, own, number, rows, number_of, top, limit, lean):
    ranking = jax.random.permutation(own_key, number_of)
    crowded, ordinary = shares(number_of, rows * top, limit, lean, True), shares(number_of, rows * top, limit, lean, False)
    places = jnp.arange(number_of)

    def named(lengths, turn):
        used = int((lengths > 0).sum())
        fixed = max(1, used // 4)
        passed = fixed + (places - fixed + turn * (used - fixed)) % max(1, number_of - fixed)
        return jnp.zeros((number_of,), jnp.int32).at[ranking[jnp.where(places < fixed, places, passed)]].set(jnp.asarray(lengths, jnp.int32))

    lengths = jnp.where(number % 4 == 0, named(crowded, number // 4), named(ordinary, number - number // 4 - 1))
    mixed = jax.random.permutation(jax.random.fold_in(own, 3), number_of)
    donor, receiver = mixed[0:number_of // 2 * 2:2], mixed[1:number_of // 2 * 2:2]
    slack = jnp.minimum(lengths[donor] - 1, limit - lengths[receiver]) // 2
    slack = jnp.where((donor == ranking[0]) | (receiver == ranking[0]) | (lengths[receiver] == 0), 0, jnp.maximum(slack, 0))
    passed = jax.random.randint(jax.random.fold_in(own, 4), (number_of // 2,), 0, 1 << 20) % (slack + 1)
    lengths = lengths.at[donor].add(-passed).at[receiver].add(passed)
    labels = jnp.searchsorted(jnp.cumsum(lengths), jnp.arange(rows * top), side="right").astype(jnp.int32)
    listing = labels.reshape(top, rows).T
    listing = listing[jax.random.permutation(jax.random.fold_in(own, 1), rows)]
    turn = jax.random.randint(jax.random.fold_in(own, 2), (rows, 1), 0, top)
    return jnp.take_along_axis(listing, (jnp.arange(top)[None, :] + turn) % top, axis=1)


def shares(amount, total, reach, slope, full):
    weights = [(1 << 20) // math.isqrt(rank ** slope) + 1 for rank in range(1, amount + 1)]
    largest = reach if full else min(reach, max(-(-total // amount), total * weights[0] // sum(weights)))
    least = 1 if total - largest >= amount - 1 else 0
    holding, spare = [largest] + [least] * (amount - 1), total - largest - least * (amount - 1)
    while spare > 0:
        free = [i for i in range(1, amount) if holding[i] < largest] or [i for i in range(1, amount) if holding[i] < reach]
        whole, budget = sum([weights[i] for i in free]), spare
        for i in free:
            more = min(reach - holding[i], max(1, budget * weights[i] // whole), spare)
            holding[i] = holding[i] + more
            spare = spare - more
    return np.array(holding)


def centred(rng, shape, deviation, most, shards=(), held_as=jnp.bfloat16):
    values = deviation * jax.random.normal(rng, shape, jnp.float32)
    if shards:
        values = values * steps_of(rng, shape, shards, -0.22, 0.18)
    return jnp.clip(values, -most, most).astype(held_as)


def setup_inputs(seed: int = 0) -> dict:
    key_of = jax.random.split(jax.random.key(seed), 8)
    tokens_in = centred(key_of[0], (TOKENS, D), 1.0, 6.0, ((0, 32),))
    grad_out = centred(key_of[1], (TOKENS, D), 1.0, 6.0, ((0, 32),))
    expert_ids_keys = jax.random.split(jax.random.fold_in(key_of[2], 1), TOKENS // TOK_DEV)
    expert_ids_turns = jax.random.permutation(jax.random.fold_in(key_of[2], 3), TOKENS // TOK_DEV)
    expert_ids = jax.vmap(lambda own, number: deal_out(jax.random.fold_in(key_of[2], 2), own, number, TOK_DEV, EXPERTS, 2, CAP, 2))(expert_ids_keys, expert_ids_turns).reshape((TOKENS, 2))
    combine = jnp.clip(0.2 + 0.8 * jax.random.uniform(key_of[3], (TOKENS, 2), jnp.float32) ** steps_of(key_of[3], (TOKENS, 2), ((0, 32),), -0.2, 0.2), 0.2, 1.0)
    w_gate = centred(key_of[4], (EXPERTS, D, FF), D ** -0.5, 0.109375, ((0, 4), (2, 8)))
    w_up = centred(key_of[5], (EXPERTS, D, FF), D ** -0.5, 0.109375, ((0, 4), (2, 8)))
    w_down = centred(key_of[6], (EXPERTS, FF, D), FF ** -0.5, 0.0625, ((0, 4), (1, 8)))
    return dict(tokens_in=tokens_in, grad_out=grad_out, expert_ids=expert_ids, combine=combine, w_gate=w_gate, w_up=w_up, w_down=w_down)


def positions(block_ids, groups):
    flat_ids = block_ids.reshape(-1)
    matches = (flat_ids[:, None] == jnp.arange(groups, dtype=jnp.int32)[None, :]).astype(jnp.int32)
    earlier = jnp.cumsum(matches, axis=0) - matches
    return jnp.sum(earlier * matches, axis=1).astype(jnp.int32)


def reference(tokens_in, grad_out, expert_ids, combine, w_gate, w_up, w_down):
    blocks = TOKENS // TOK_DEV
    pairs = TOKENS * 2
    buffer_rows = blocks * CAP
    slots = jax.vmap(lambda span_ids: positions(span_ids, EXPERTS))(expert_ids.reshape(blocks, TOK_DEV, 2)).reshape(-1)
    flat_ids = expert_ids.reshape(-1)
    pair_index = jnp.arange(pairs, dtype=jnp.int32)
    token_of = pair_index // 2
    block_of = token_of // TOK_DEV
    scaled = (combine[:, :, None] * grad_out.astype(jnp.float32)[:, None, :]).astype(jnp.bfloat16).reshape(pairs, D)

    def one_expert(packed):
        number, gate_w, up_w, down_w = packed
        target = jnp.where(flat_ids == number, block_of * CAP + slots, buffer_rows).astype(jnp.int32)
        source = jnp.full((buffer_rows,), pairs, jnp.int32).at[target].set(pair_index, mode="drop")
        valid = source < pairs
        safe = jnp.minimum(source, pairs - 1)
        rows_in = jnp.where(valid[:, None], tokens_in[safe // 2], jnp.zeros((), jnp.bfloat16))
        rows_grad = jnp.where(valid[:, None], scaled[safe], jnp.zeros((), jnp.bfloat16))
        gate_pre = jnp.dot(rows_in, gate_w, preferred_element_type=jnp.float32)
        up_pre = jnp.dot(rows_in, up_w, preferred_element_type=jnp.float32)
        sigmoid_gate = jax.nn.sigmoid(gate_pre)
        activated = gate_pre * sigmoid_gate
        hidden = (activated * up_pre).astype(jnp.bfloat16)
        grad_down = jnp.dot(hidden.T, rows_grad, preferred_element_type=jnp.float32).astype(jnp.bfloat16)
        grad_hidden = jnp.dot(rows_grad, down_w.T, preferred_element_type=jnp.float32)
        grad_gate_pre = (grad_hidden * up_pre * sigmoid_gate * (1.0 + gate_pre * (1.0 - sigmoid_gate))).astype(jnp.bfloat16)
        grad_up_pre = (grad_hidden * activated).astype(jnp.bfloat16)
        grad_gate = jnp.dot(rows_in.T, grad_gate_pre, preferred_element_type=jnp.float32).astype(jnp.bfloat16)
        grad_up = jnp.dot(rows_in.T, grad_up_pre, preferred_element_type=jnp.float32).astype(jnp.bfloat16)
        rows_back = (jnp.dot(grad_gate_pre, gate_w.T, preferred_element_type=jnp.float32)
                     + jnp.dot(grad_up_pre, up_w.T, preferred_element_type=jnp.float32)).astype(jnp.bfloat16)
        owner = jnp.where(valid, safe // 2, TOKENS).astype(jnp.int32)
        return grad_gate, grad_up, grad_down, rows_back, owner

    numbers = jnp.arange(EXPERTS, dtype=jnp.int32)
    grad_gate, grad_up, grad_down, rows_back, owner = lax.map(one_expert, (numbers, w_gate, w_up, w_down))
    summed = jnp.zeros((TOKENS + 1, D), jnp.float32).at[owner.reshape(-1)].add(rows_back.reshape(-1, D).astype(jnp.float32))
    grad_input = summed[:TOKENS].astype(jnp.bfloat16)
    return grad_input, grad_gate, grad_up, grad_down
```

```python
import functools

import jax
import jax.numpy as jnp
from jax import lax
from jax.experimental import pallas as pl
from jax.experimental.pallas import tpu as pltpu
from jax.sharding import PartitionSpec as P

F32, BF16 = jnp.float32, jnp.bfloat16
PIECES = 3
VMEM_BYTES = 60 * 1024 * 1024


def dot(left, right, on_left, on_right):
    return lax.dot_general(
        left, right, (((on_left,), (on_right,)), ((), ())), preferred_element_type=F32
    )


def routing(meta, experts, rows, tokens):
    slots = tokens // 4
    extent = (rows, tokens)
    row = lax.broadcasted_iota(jnp.int32, extent, 0)
    lane = lax.broadcasted_iota(jnp.int32, extent, 1)
    unit = jnp.zeros(extent, jnp.int32)
    for i in range(1, 2 * experts):
        unit = unit + (row >= i * slots).astype(jnp.int32)
    slot = (row - unit * slots).astype(F32)
    core = unit & 1
    expert = (unit >> 1).astype(F32)
    same = (core == (lane >= tokens // 2).astype(jnp.int32)).astype(F32)
    first = (meta[0:1, :tokens] == expert).astype(F32) * same
    second = (meta[1:2, :tokens] == expert).astype(F32) * same
    named = first + second
    before = lax.broadcasted_iota(jnp.int32, (tokens, tokens), 0) < lax.broadcasted_iota(
        jnp.int32, (tokens, tokens), 1
    )
    earlier = dot(named.astype(BF16), before.astype(F32).astype(BF16), 1, 0)
    picks = named * (earlier == slot).astype(F32)
    weight = jnp.sum(
        picks * (first * meta[2:3, :tokens] + second * meta[3:4, :tokens]), axis=1, keepdims=True
    )
    return picks, weight


def exchange(E, C, tok, grad, meta, wg_h, wu_h, wd_h,
             rin_o, rgr_o, hid_o, ggp_o, gup_o, gi_o,
             wg, wu, wd, swap, gath, metab, sendb, X, picks, hid, ggp, gup,
             sibs, sibr, part, ret, tokp, zr, fin, got,
             wsem, osem, sw_s, sw_r, ga_s, ga_r, me_s, me_r, ex_s, ex_r, sx_s, sx_r,
             si_s, si_r, pa_s, pa_r, to_s, to_r, fi_s, fi_r):
    n_tok, D = tok.shape
    R = C * E * n_tok
    F = wg.shape[1]
    W = D // 2
    cw = W // PIECES
    e = lax.axis_index("expert")
    t = lax.axis_index("tp")
    z, c = t // 2, t % 2
    o = 1 - c

    def remote(src, dst, ssem, rsem, expert, tp):
        return pltpu.make_async_remote_copy(
            src_ref=src, dst_ref=dst, send_sem=ssem, recv_sem=rsem,
            device_id={"expert": expert, "tp": tp}, device_id_type=pl.DeviceIdType.MESH)

    sib = z * 2 + o
    weights = [pltpu.make_async_copy(a.at[0], b, wsem.at[i])
               for i, (a, b) in enumerate(((wg_h, wg), (wu_h, wu), (wd_h, wd)))]
    for w in weights:
        w.start()

    peers = [lax.rem(e + i, E) for i in range(1, E)]
    chips = [lax.rem(z + i, C) for i in range(1, C)]
    barrier = pltpu.get_barrier_semaphore()

    def hello(expert, tp):
        pl.semaphore_signal(barrier, inc=1, device_id={"expert": expert, "tp": tp},
                            device_id_type=pl.DeviceIdType.MESH)
    hello(e, sib)
    for q in peers:
        hello(q, t)
    for q in chips:
        hello(e, q * 2 + c)
    pl.semaphore_wait(barrier, 1 + (E - 1) + (C - 1))

    is_in = c == 0
    swap[...] = jnp.where(is_in, grad[...].astype(F32), tok[...].astype(F32)).astype(BF16)
    gath[z, c] = jnp.where(is_in, tok[...].astype(F32), grad[...].astype(F32)).astype(BF16)
    metab[z, c] = meta[...]
    a = remote(swap, gath.at[z, c], sw_s.at[0], sw_r.at[0], e, sib)
    b = remote(metab.at[z, c], metab.at[z, c], sw_s.at[1], sw_r.at[1], e, sib)
    a.start()
    b.start()
    a.wait_recv()
    b.wait_recv()

    def hop(origin, way):
        tp = (z + (1 if way == 0 else -1)) * 2 + c
        return (remote(gath.at[origin], gath.at[origin], ga_s.at[origin, way], ga_r.at[origin], e, tp),
                remote(metab.at[origin], metab.at[origin], me_s.at[origin, way], me_r.at[origin], e, tp))

    def send_on(origin, way):
        for d in hop(origin, way):
            d.start()

    can = (z + 1 < C, z >= 1)
    for way in (0, 1):
        pl.when(can[way])(functools.partial(send_on, z, way))

    def rows_out(origin, i):
        return remote(sendb.at[origin, peers[i]], X.at[c, origin, e],
                      ex_s.at[origin, i], ex_r.at[origin, i], peers[i], t)

    def process(origin):
        info = metab[origin, 0] + metab[origin, 1]
        sel, weight = routing(info, E, E * n_tok, 2 * n_tok)
        sel = sel.astype(BF16)
        picks[origin] = sel
        scale = jnp.where(is_in, jnp.ones_like(weight), weight)
        rows = dot(sel, gath[origin].reshape(2 * n_tok, D), 1, 0)
        sendb[origin] = (rows * scale).astype(BF16).reshape(E, n_tok, D)
        for i in range(E - 1):
            rows_out(origin, i).start()
        X[c, origin, e] = sendb[origin, e]

    def sibling_rows(kind, origin):
        return remote(X.at[kind, origin], X.at[kind, origin], sx_s.at[origin], sx_r.at[origin], e, sib)

    def arrived(origin):
        for i in range(E - 1):
            rows_out(origin, i).wait_recv()
        sibling_rows(c, origin).start()

    def take(origin, way):
        for d in hop(origin, way):
            d.wait_recv()
        pl.when(can[way])(functools.partial(send_on, origin, way))
        process(origin)

    process(z)
    for k in range(1, C):
        pl.when(z - k >= 0)(functools.partial(take, z - k, 0))
        pl.when(z + k < C)(functools.partial(take, z + k, 1))
    arrived(z)
    for k in range(1, C):
        pl.when(z - k >= 0)(functools.partial(arrived, z - k))
        pl.when(z + k < C)(functools.partial(arrived, z + k))
    for q in range(C):
        sibling_rows(o, q).wait_recv()
    for w in weights:
        w.wait()

    saves = [pltpu.make_async_copy(X.at[0], rin_o, osem.at[0]),
             pltpu.make_async_copy(X.at[1], rgr_o, osem.at[1])]
    for s in saves:
        s.start()

    step = min(256, F)

    @pl.loop(0, F // step)
    def _(n):
        cols = pl.ds(pl.multiple_of(n * step, step), step)
        rin = X[0].reshape(R, D)
        rgr = X[1].reshape(R, D)
        gate = dot(rin, wg[:, cols], 1, 0)
        up = dot(rin, wu[:, cols], 1, 0)
        gh = dot(rgr, wd[cols, :], 1, 1)
        s = jax.nn.sigmoid(gate)
        act = gate * s
        hid[:, cols] = (act * up).astype(BF16)
        ggp[:, cols] = (gh * up * s * (1.0 + gate * (1.0 - s))).astype(BF16)
        gup[:, cols] = (gh * act).astype(BF16)

    more = [pltpu.make_async_copy(a, b, osem.at[2 + i])
            for i, (a, b) in enumerate(((hid, hid_o), (ggp, ggp_o), (gup, gup_o)))]
    for s in more:
        s.start()
    saves += more

    def back(half, n):
        at = pl.ds(pl.multiple_of(half * W + n * cw, cw), cw)
        return dot(ggp[...], wg[at, :], 1, 1) + dot(gup[...], wu[at, :], 1, 1)

    def sib_sum(n):
        return remote(sibs.at[n], sibr.at[n], si_s.at[n], si_r.at[n], e, sib)

    def part_out(n, i):
        return remote(part.at[n, :, peers[i]], ret.at[n, e], pa_s.at[n, i], pa_r.at[n, i], peers[i], t)

    def tok_out(n, i):
        return remote(tokp.at[n, chips[i]], zr.at[n, z], to_s.at[n, i], to_r.at[n, i], e, chips[i] * 2 + c)

    def fin_out(n):
        return remote(fin.at[n, o], got.at[n], fi_s.at[n], fi_r.at[n], e, sib)

    for n in range(PIECES):
        sibs[n] = back(o, n).astype(BF16)
        sib_sum(n).start()
    for n in range(PIECES):
        own = back(c, n)
        sib_sum(n).wait_recv()
        part[n] = (own + sibr[n].astype(F32)).astype(BF16).reshape(C, E, n_tok, cw)
        for i in range(E - 1):
            part_out(n, i).start()
        ret[n, e] = part[n, :, e]

    def to_tokens(n, q):
        return dot(picks[q], ret[n, :, q].reshape(E * n_tok, cw), 0, 0)

    for n in range(PIECES):
        for i in range(E - 1):
            part_out(n, i).wait_recv()
        for i in range(C - 1):
            tokp[n, chips[i]] = to_tokens(n, chips[i]).astype(BF16).reshape(2, n_tok, cw)
            tok_out(n, i).start()
    for n in range(PIECES):
        total = to_tokens(n, z)
        for i in range(C - 1):
            tok_out(n, i).wait_recv()
        for i in range(C - 1):
            total = total + zr[n, chips[i]].astype(F32).reshape(2 * n_tok, cw)
        fin[n] = total.astype(BF16).reshape(2, n_tok, cw)
        fin_out(n).start()
        gi_o[:, pl.ds(pl.multiple_of(c * W + n * cw, cw), cw)] = fin[n, c]
    for n in range(PIECES):
        fin_out(n).wait_recv()
        gi_o[:, pl.ds(pl.multiple_of(o * W + n * cw, cw), cw)] = got[n]

    a.wait_send()
    b.wait_send()

    def sent(origin, way):
        for d in hop(origin, way):
            d.wait_send()

    for way in (0, 1):
        pl.when(can[way])(functools.partial(sent, z, way))
    for k in range(1, C):
        pl.when(jnp.logical_and(z - k >= 0, can[0]))(functools.partial(sent, z - k, 0))
        pl.when(jnp.logical_and(z + k < C, can[1]))(functools.partial(sent, z + k, 1))
    for q in range(C):
        for i in range(E - 1):
            rows_out(q, i).wait_send()
        sibling_rows(c, q).wait_send()
    for n in range(PIECES):
        sib_sum(n).wait_send()
        for i in range(E - 1):
            part_out(n, i).wait_send()
        for i in range(C - 1):
            tok_out(n, i).wait_send()
        fin_out(n).wait_send()
    for s in saves:
        s.wait()


def weight_grads(rin, rgr, hid, ggp, gup, gg, gu, gd):
    x = rin[...]
    gg[0] = dot(x, ggp[...], 0, 0).astype(BF16)
    gu[0] = dot(x, gup[...], 0, 0).astype(BF16)
    gd[0] = dot(hid[...], rgr[...], 0, 0).astype(BF16)


def per_device(E, T, tokens_in, grad_out, expert_ids, combine, w_gate, w_up, w_down):
    n_tok, D = tokens_in.shape
    F = w_gate.shape[2]
    C = T // 2
    R = C * E * n_tok
    cw = D // 2 // PIECES
    small = jnp.concatenate([expert_ids.T.astype(F32), combine.T], axis=0)
    core = lax.axis_index("tp") % 2
    wide = jnp.concatenate([jnp.where(core == 0, small, 0.0), jnp.where(core == 1, small, 0.0)], axis=1)
    meta = jnp.pad(wide, ((0, 4), (0, 128 - 2 * n_tok)))
    any_, vm = pl.BlockSpec(memory_space=pl.ANY), pl.BlockSpec(memory_space=pltpu.VMEM)
    rows_t = jax.ShapeDtypeStruct((C, E, n_tok, D), BF16)
    ff_t = jax.ShapeDtypeStruct((R, F), BF16)
    V, S = pltpu.VMEM, pltpu.SemaphoreType.DMA
    rin, rgr, hid, ggp, gup, grad_input = pl.pallas_call(
        functools.partial(exchange, E, C),
        out_shape=(rows_t, rows_t, ff_t, ff_t, ff_t, jax.ShapeDtypeStruct((n_tok, D), BF16)),
        in_specs=[vm, vm, vm, any_, any_, any_],
        out_specs=(any_, any_, any_, any_, any_, vm),
        scratch_shapes=[
            V((D, F), BF16), V((D, F), BF16), V((F, D), BF16),
            V((n_tok, D), BF16), V((C, 2, n_tok, D), BF16), V((C, 2, 8, 128), F32),
            V((C, E, n_tok, D), BF16), V((2, C, E, n_tok, D), BF16),
            V((C, E * n_tok, 2 * n_tok), BF16),
            V((R, F), BF16), V((R, F), BF16), V((R, F), BF16),
            V((PIECES, R, cw), BF16), V((PIECES, R, cw), BF16),
            V((PIECES, C, E, n_tok, cw), BF16), V((PIECES, E, C, n_tok, cw), BF16),
            V((PIECES, C, 2, n_tok, cw), BF16), V((PIECES, C, 2, n_tok, cw), BF16),
            V((PIECES, 2, n_tok, cw), BF16), V((PIECES, n_tok, cw), BF16),
            S((3,)), S((5,)), S((2,)), S((2,)),
            S((C, 2)), S((C,)), S((C, 2)), S((C,)),
            S((C, E - 1)), S((C, E - 1)), S((C,)), S((C,)),
            S((PIECES,)), S((PIECES,)), S((PIECES, E - 1)), S((PIECES, E - 1)),
            S((PIECES, C - 1)), S((PIECES, C - 1)), S((PIECES,)), S((PIECES,)),
        ],
        compiler_params=pltpu.CompilerParams(
            collective_id=0, has_side_effects=True, vmem_limit_bytes=VMEM_BYTES),
        cost_estimate=pl.CostEstimate(
            flops=10 * R * D * F, bytes_accessed=6 * D * F, transcendentals=R * F),
        name="exchange",
    )(tokens_in, grad_out, meta, w_gate, w_up, w_down)
    block = 512
    whole = pl.BlockSpec((R, F), lambda i: (0, 0))
    cols = pl.BlockSpec((R, block), lambda i: (0, i))
    gg, gu, gd = pl.pallas_call(
        weight_grads,
        grid=(D // block,),
        out_shape=(jax.ShapeDtypeStruct((1, D, F), BF16), jax.ShapeDtypeStruct((1, D, F), BF16),
                   jax.ShapeDtypeStruct((1, F, D), BF16)),
        in_specs=[cols, cols, whole, whole, whole],
        out_specs=(pl.BlockSpec((1, block, F), lambda i: (0, i, 0)),
                   pl.BlockSpec((1, block, F), lambda i: (0, i, 0)),
                   pl.BlockSpec((1, F, block), lambda i: (0, 0, i))),
        compiler_params=pltpu.CompilerParams(vmem_limit_bytes=VMEM_BYTES // 2),
        cost_estimate=pl.CostEstimate(
            flops=6 * R * D * F, bytes_accessed=6 * D * F, transcendentals=0),
        name="weight_grads",
    )(rin.reshape(R, D), rgr.reshape(R, D), hid, ggp, gup)
    return grad_input, gg, gu, gd


def solution(mesh):
    rows = P(("expert", "tp"), None)
    columns = P("expert", None, "tp")
    return jax.shard_map(
        functools.partial(per_device, mesh.shape["expert"], mesh.shape["tp"]),
        mesh=mesh,
        in_specs=(rows, rows, rows, rows, columns, columns, P("expert", "tp", None)),
        out_specs=(rows, columns, columns, P("expert", "tp", None)),
        check_vma=False,
    )
```

```python
import functools

import jax
import jax.numpy as jnp
from jax import lax
from jax.experimental import pallas as pl
from jax.experimental.pallas import tpu as pltpu
from jax.sharding import PartitionSpec as P

F32, BF16 = jnp.float32, jnp.bfloat16
PIECES = 3
VMEM_BYTES = 60 * 1024 * 1024


def dot(left, right, on_left, on_right):
    return lax.dot_general(
        left, right, (((on_left,), (on_right,)), ((), ())), preferred_element_type=F32
    )


def routing(meta, experts, rows, tokens):
    slots = tokens // 4
    extent = (rows, tokens)
    row = lax.broadcasted_iota(jnp.int32, extent, 0)
    lane = lax.broadcasted_iota(jnp.int32, extent, 1)
    unit = jnp.zeros(extent, jnp.int32)
    for i in range(1, 2 * experts):
        unit = unit + (row >= i * slots).astype(jnp.int32)
    slot = (row - unit * slots).astype(F32)
    core = unit & 1
    expert = (unit >> 1).astype(F32)
    same = (core == (lane >= tokens // 2).astype(jnp.int32)).astype(F32)
    first = (meta[0:1, :tokens] == expert).astype(F32) * same
    second = (meta[1:2, :tokens] == expert).astype(F32) * same
    named = first + second
    before = lax.broadcasted_iota(jnp.int32, (tokens, tokens), 0) < lax.broadcasted_iota(
        jnp.int32, (tokens, tokens), 1
    )
    earlier = dot(named.astype(BF16), before.astype(F32).astype(BF16), 1, 0)
    picks = named * (earlier == slot).astype(F32)
    weight = jnp.sum(
        picks * (first * meta[2:3, :tokens] + second * meta[3:4, :tokens]), axis=1, keepdims=True
    )
    return picks, weight


def exchange(E, C, tok, grad, ids, comb, wg_h, wu_h, wd_h,
             rin_o, rgr_o, hid_o, ggp_o, gup_o, gi_o,
             wg, wu, wd, swap, gath, metab, sendb, X, picks, hid, ggp, gup, rin_t, hid_t,
             sibs, sibr, part, ret, tokp, zr, fin, got,
             wsem, osem, sw_s, sw_r, ga_s, ga_r, me_s, me_r, ex_s, ex_r, sx_s, sx_r,
             si_s, si_r, pa_s, pa_r, to_s, to_r, fi_s, fi_r):
    n_tok, D = tok.shape
    R = C * E * n_tok
    F = wg.shape[1]
    W = D // 2
    cw = W // PIECES
    e = lax.axis_index("expert")
    t = lax.axis_index("tp")
    z, c = t // 2, t % 2
    o = 1 - c

    def remote(src, dst, ssem, rsem, expert, tp):
        return pltpu.make_async_remote_copy(
            src_ref=src, dst_ref=dst, send_sem=ssem, recv_sem=rsem,
            device_id={"expert": expert, "tp": tp}, device_id_type=pl.DeviceIdType.MESH)

    sib = z * 2 + o
    is_in = c == 0
    weights = [pltpu.make_async_copy(a.at[0], b, wsem.at[i])
               for i, (a, b) in enumerate(((wg_h, wg), (wu_h, wu), (wd_h, wd)))]
    for w in weights:
        w.start()

    peers = [lax.rem(e + i, E) for i in range(1, E)]
    chips = [lax.rem(z + i, C) for i in range(1, C)]
    barrier = pltpu.get_barrier_semaphore()

    def hello(expert, tp):
        pl.semaphore_signal(barrier, inc=1, device_id={"expert": expert, "tp": tp},
                            device_id_type=pl.DeviceIdType.MESH)
    hello(e, sib)
    for q in peers:
        hello(q, t)
    for q in chips:
        hello(e, q * 2 + c)
    pl.semaphore_wait(barrier, 1 + (E - 1) + (C - 1))

    swap[...] = jnp.where(is_in, grad[...].astype(F32), tok[...].astype(F32)).astype(BF16)
    gath[z, c] = jnp.where(is_in, tok[...].astype(F32), grad[...].astype(F32)).astype(BF16)
    metab[z, c] = jnp.zeros((8, 128), F32)
    for i, source in enumerate((ids, comb)):
        values = source[...].astype(F32)
        none = jnp.zeros_like(values)
        metab[z, c, 2 * i:2 * i + 2, :2 * n_tok] = jnp.concatenate(
            [jnp.where(is_in, values, none), jnp.where(is_in, none, values)], axis=1)

    near = jnp.minimum(z, C - 1 - z)

    def position(origin):
        far = jnp.abs(origin - z)
        return jnp.where(far <= near, jnp.where(origin < z, 2 * far - 1, 2 * far), near + far)
    a = remote(swap, gath.at[z, c], sw_s.at[0], sw_r.at[0], e, sib)
    b = remote(metab.at[z, c], metab.at[z, c], sw_s.at[1], sw_r.at[1], e, sib)
    a.start()
    b.start()
    a.wait_recv()
    b.wait_recv()

    def hop(origin, way):
        tp = (z + (1 if way == 0 else -1)) * 2 + c
        return (remote(gath.at[origin], gath.at[origin], ga_s.at[origin, way], ga_r.at[origin], e, tp),
                remote(metab.at[origin], metab.at[origin], me_s.at[origin, way], me_r.at[origin], e, tp))

    def send_on(origin, way):
        for d in hop(origin, way):
            d.start()

    can = (z + 1 < C, z >= 1)
    for way in (0, 1):
        pl.when(can[way])(functools.partial(send_on, z, way))

    def rows_out(origin, i, m):
        return remote(sendb.at[origin, peers[i]], X.at[c, m, e],
                      ex_s.at[origin, i], ex_r.at[m, i], peers[i], t)

    def process(origin):
        info = metab[origin, 0] + metab[origin, 1]
        sel, weight = routing(info, E, E * n_tok, 2 * n_tok)
        sel = sel.astype(BF16)
        picks[origin] = sel
        scale = jnp.where(is_in, jnp.ones_like(weight), weight)
        rows = dot(sel, gath[origin].reshape(2 * n_tok, D), 1, 0)
        sendb[origin] = (rows * scale).astype(BF16).reshape(E, n_tok, D)
        for i in range(E - 1):
            rows_out(origin, i, position(origin)).start()
        X[c, position(origin), e] = sendb[origin, e]

    def sibling_rows(kind, m):
        return remote(X.at[kind, m], X.at[kind, m], sx_s.at[m], sx_r.at[m], e, sib)

    def arrived(m):
        for i in range(E - 1):
            rows_out(0, i, m).wait_recv()
        sibling_rows(c, m).start()

    def take(origin, way):
        for d in hop(origin, way):
            d.wait_recv()
        pl.when(can[way])(functools.partial(send_on, origin, way))
        process(origin)

    process(z)
    for k in range(1, C):
        pl.when(z - k >= 0)(functools.partial(take, z - k, 0))
        pl.when(z + k < C)(functools.partial(take, z + k, 1))
    step = min(256, F)
    part_rows = C // 2
    half_rows = R // 2

    def hidden_units(h):
        for m in range(h * part_rows, (h + 1) * part_rows):
            sibling_rows(o, m).wait_recv()
        rows = pl.ds(h * half_rows, half_rows)

        @pl.loop(0, F // step)
        def _(n):
            cols = pl.ds(pl.multiple_of(n * step, step), step)
            rin = X[0, pl.ds(h * part_rows, part_rows)].reshape(half_rows, D)
            rgr = X[1, pl.ds(h * part_rows, part_rows)].reshape(half_rows, D)
            gate = dot(rin, wg[:, cols], 1, 0)
            up = dot(rin, wu[:, cols], 1, 0)
            gh = dot(rgr, wd[cols, :], 1, 1)
            s = jax.nn.sigmoid(gate)
            act = gate * s
            hid[rows, cols] = (act * up).astype(BF16)
            ggp[rows, cols] = (gh * up * s * (1.0 + gate * (1.0 - s))).astype(BF16)
            gup[rows, cols] = (gh * act).astype(BF16)

    for m in range(part_rows):
        arrived(m)
    for w in weights:
        w.wait()
    hidden_units(0)
    for m in range(part_rows, C):
        arrived(m)
    hidden_units(1)

    saves = [pltpu.make_async_copy(a, b, osem.at[i])
             for i, (a, b) in enumerate(((X.at[1], rgr_o), (ggp, ggp_o), (gup, gup_o)))]
    for s in saves:
        s.start()

    def back(half, n):
        at = pl.ds(pl.multiple_of(half * W + n * cw, cw), cw)
        return dot(ggp[...], wg[at, :], 1, 1) + dot(gup[...], wu[at, :], 1, 1)

    def sib_sum(n):
        return remote(sibs.at[n], sibr.at[n], si_s.at[n], si_r.at[n], e, sib)

    def part_out(n, i):
        return remote(part.at[n, :, peers[i]], ret.at[n, e], pa_s.at[n, i], pa_r.at[n, i], peers[i], t)

    def tok_out(n, i):
        return remote(tokp.at[n, chips[i]], zr.at[n, z], to_s.at[n, i], to_r.at[n, i], e, chips[i] * 2 + c)

    def fin_out(n):
        return remote(fin.at[n, o], got.at[n], fi_s.at[n], fi_r.at[n], e, sib)

    for n in range(PIECES):
        sibs[n] = back(o, n).astype(BF16)
        sib_sum(n).start()
    for n in range(PIECES):
        own = back(c, n)
        sib_sum(n).wait_recv()
        part[n] = (own + sibr[n].astype(F32)).astype(BF16).reshape(C, E, n_tok, cw)
        for i in range(E - 1):
            part_out(n, i).start()
        ret[n, e] = part[n, :, e]

    @pl.loop(0, D // 256)
    def _(n):
        at = pl.ds(pl.multiple_of(n * 256, 256), 256)
        rin_t[at, :] = X[0, :, :, :, at].reshape(R, 256).T

    @pl.loop(0, F // 256)
    def _(n):
        at = pl.ds(pl.multiple_of(n * 256, 256), 256)
        hid_t[at, :] = hid[:, at].T

    turned = [pltpu.make_async_copy(a, b, osem.at[3 + i])
              for i, (a, b) in enumerate(((rin_t, rin_o), (hid_t, hid_o)))]
    for s in turned:
        s.start()
    saves += turned

    def to_tokens(n, q):
        return dot(picks[q], ret[n, :, position(q)].reshape(E * n_tok, cw), 0, 0)

    for n in range(PIECES):
        for i in range(E - 1):
            part_out(n, i).wait_recv()
        for i in range(C - 1):
            tokp[n, chips[i]] = to_tokens(n, chips[i]).astype(BF16).reshape(2, n_tok, cw)
            tok_out(n, i).start()
    for n in range(PIECES):
        total = to_tokens(n, z)
        for i in range(C - 1):
            tok_out(n, i).wait_recv()
        for i in range(C - 1):
            total = total + zr[n, chips[i]].astype(F32).reshape(2 * n_tok, cw)
        fin[n] = total.astype(BF16).reshape(2, n_tok, cw)
        fin_out(n).start()
        gi_o[:, pl.ds(pl.multiple_of(c * W + n * cw, cw), cw)] = fin[n, c]
    for n in range(PIECES):
        fin_out(n).wait_recv()
        gi_o[:, pl.ds(pl.multiple_of(o * W + n * cw, cw), cw)] = got[n]

    a.wait_send()
    b.wait_send()

    def sent(origin, way):
        for d in hop(origin, way):
            d.wait_send()

    for way in (0, 1):
        pl.when(can[way])(functools.partial(sent, z, way))
    for k in range(1, C):
        pl.when(jnp.logical_and(z - k >= 0, can[0]))(functools.partial(sent, z - k, 0))
        pl.when(jnp.logical_and(z + k < C, can[1]))(functools.partial(sent, z + k, 1))
    for q in range(C):
        for i in range(E - 1):
            rows_out(q, i, q).wait_send()
        sibling_rows(c, q).wait_send()
    for n in range(PIECES):
        sib_sum(n).wait_send()
        for i in range(E - 1):
            part_out(n, i).wait_send()
        for i in range(C - 1):
            tok_out(n, i).wait_send()
        fin_out(n).wait_send()
    for s in saves:
        s.wait()


def weight_grads(rin, rgr, hid, ggp, gup, gg, gu, gd):
    x = rin[...]
    gg[0] = dot(x, ggp[...], 1, 0).astype(BF16)
    gu[0] = dot(x, gup[...], 1, 0).astype(BF16)
    gd[0] = dot(hid[...], rgr[...], 1, 0).astype(BF16)


def per_device(E, T, tokens_in, grad_out, expert_ids, combine, w_gate, w_up, w_down):
    n_tok, D = tokens_in.shape
    F = w_gate.shape[2]
    C = T // 2
    R = C * E * n_tok
    cw = D // 2 // PIECES
    any_, vm = pl.BlockSpec(memory_space=pl.ANY), pl.BlockSpec(memory_space=pltpu.VMEM)
    rows_t = jax.ShapeDtypeStruct((C, E, n_tok, D), BF16)
    ff_t = jax.ShapeDtypeStruct((R, F), BF16)
    V, S = pltpu.VMEM, pltpu.SemaphoreType.DMA
    rin, rgr, hid, ggp, gup, grad_input = pl.pallas_call(
        functools.partial(exchange, E, C),
        out_shape=(jax.ShapeDtypeStruct((D, R), BF16), rows_t, jax.ShapeDtypeStruct((F, R), BF16), ff_t, ff_t, jax.ShapeDtypeStruct((n_tok, D), BF16)),
        in_specs=[vm, vm, vm, vm, any_, any_, any_],
        out_specs=(any_, any_, any_, any_, any_, vm),
        scratch_shapes=[
            V((D, F), BF16), V((D, F), BF16), V((F, D), BF16),
            V((n_tok, D), BF16), V((C, 2, n_tok, D), BF16), V((C, 2, 8, 128), F32),
            V((C, E, n_tok, D), BF16), V((2, C, E, n_tok, D), BF16),
            V((C, E * n_tok, 2 * n_tok), BF16),
            V((R, F), BF16), V((R, F), BF16), V((R, F), BF16), V((D, R), BF16), V((F, R), BF16),
            V((PIECES, R, cw), BF16), V((PIECES, R, cw), BF16),
            V((PIECES, C, E, n_tok, cw), BF16), V((PIECES, E, C, n_tok, cw), BF16),
            V((PIECES, C, 2, n_tok, cw), BF16), V((PIECES, C, 2, n_tok, cw), BF16),
            V((PIECES, 2, n_tok, cw), BF16), V((PIECES, n_tok, cw), BF16),
            S((3,)), S((5,)), S((2,)), S((2,)),
            S((C, 2)), S((C,)), S((C, 2)), S((C,)),
            S((C, E - 1)), S((C, E - 1)), S((C,)), S((C,)),
            S((PIECES,)), S((PIECES,)), S((PIECES, E - 1)), S((PIECES, E - 1)),
            S((PIECES, C - 1)), S((PIECES, C - 1)), S((PIECES,)), S((PIECES,)),
        ],
        compiler_params=pltpu.CompilerParams(
            collective_id=0, has_side_effects=True, vmem_limit_bytes=VMEM_BYTES),
        cost_estimate=pl.CostEstimate(
            flops=10 * R * D * F, bytes_accessed=6 * D * F, transcendentals=R * F),
        name="exchange",
    )(tokens_in, grad_out, expert_ids.T, combine.T, w_gate, w_up, w_down)
    block = 512
    whole = pl.BlockSpec((R, F), lambda i: (0, 0))
    cols = pl.BlockSpec((R, block), lambda i: (0, i))
    gg, gu, gd = pl.pallas_call(
        weight_grads,
        grid=(D // block,),
        out_shape=(jax.ShapeDtypeStruct((1, D, F), BF16), jax.ShapeDtypeStruct((1, D, F), BF16),
                   jax.ShapeDtypeStruct((1, F, D), BF16)),
        in_specs=[pl.BlockSpec((block, R), lambda i: (i, 0)), cols,
                  pl.BlockSpec((F, R), lambda i: (0, 0)), whole, whole],
        out_specs=(pl.BlockSpec((1, block, F), lambda i: (0, i, 0)),
                   pl.BlockSpec((1, block, F), lambda i: (0, i, 0)),
                   pl.BlockSpec((1, F, block), lambda i: (0, 0, i))),
        compiler_params=pltpu.CompilerParams(vmem_limit_bytes=VMEM_BYTES),
        cost_estimate=pl.CostEstimate(
            flops=6 * R * D * F, bytes_accessed=6 * D * F, transcendentals=0),
        name="weight_grads",
    )(rin, rgr.reshape(R, D), hid, ggp, gup)
    return grad_input, gg, gu, gd


def solution(mesh):
    rows = P(("expert", "tp"), None)
    columns = P("expert", None, "tp")
    return jax.shard_map(
        functools.partial(per_device, mesh.shape["expert"], mesh.shape["tp"]),
        mesh=mesh,
        in_specs=(rows, rows, rows, rows, columns, columns, P("expert", "tp", None)),
        out_specs=(rows, columns, columns, P("expert", "tp", None)),
        check_vma=False,
    )
```

```python
import functools

import jax
import jax.numpy as jnp
from jax import lax
from jax.experimental import pallas as pl
from jax.experimental.pallas import tpu as pltpu
from jax.sharding import PartitionSpec as P

F32, BF16 = jnp.float32, jnp.bfloat16
PIECES = 3
VMEM_BYTES = 60 * 1024 * 1024


def dot(left, right, on_left, on_right):
    return lax.dot_general(
        left, right, (((on_left,), (on_right,)), ((), ())), preferred_element_type=F32
    )


def routing(meta, experts, rows, tokens):
    slots = tokens // 4
    extent = (rows, tokens)
    row = lax.broadcasted_iota(jnp.int32, extent, 0)
    lane = lax.broadcasted_iota(jnp.int32, extent, 1)
    unit = jnp.zeros(extent, jnp.int32)
    for i in range(1, 2 * experts):
        unit = unit + (row >= i * slots).astype(jnp.int32)
    slot = (row - unit * slots).astype(F32)
    core = unit & 1
    expert = (unit >> 1).astype(F32)
    same = (core == (lane >= tokens // 2).astype(jnp.int32)).astype(F32)
    first = (meta[0:1, :tokens] == expert).astype(F32) * same
    second = (meta[1:2, :tokens] == expert).astype(F32) * same
    named = first + second
    before = lax.broadcasted_iota(jnp.int32, (tokens, tokens), 0) < lax.broadcasted_iota(
        jnp.int32, (tokens, tokens), 1
    )
    earlier = dot(named.astype(BF16), before.astype(F32).astype(BF16), 1, 0)
    picks = named * (earlier == slot).astype(F32)
    weight = jnp.sum(
        picks * (first * meta[2:3, :tokens] + second * meta[3:4, :tokens]), axis=1, keepdims=True
    )
    return picks, weight


def exchange(E, C, tok, grad, ids, comb, wg_h, wu_h, wd_h,
             rin_o, rgr_o, hid_o, ggp_o, gup_o, gi_o,
             wg, wu, wd, swap, gath, metab, sendb, X, picks, hid, ggp, gup, rin_t, hid_t,
             sibs, sibr, part, ret, tokp, zr, fin, got,
             wsem, osem, sw_s, sw_r, ga_s, ga_r, me_s, me_r, ex_s, ex_r, sx_s, sx_r,
             si_s, si_r, pa_s, pa_r, to_s, to_r, fi_s, fi_r):
    n_tok, D = tok.shape
    R = C * E * n_tok
    F = wg.shape[1]
    W = D // 2
    cw = W // PIECES
    e = lax.axis_index("expert")
    t = lax.axis_index("tp")
    z, c = t // 2, t % 2
    o = 1 - c

    def remote(src, dst, ssem, rsem, expert, tp):
        return pltpu.make_async_remote_copy(
            src_ref=src, dst_ref=dst, send_sem=ssem, recv_sem=rsem,
            device_id={"expert": expert, "tp": tp}, device_id_type=pl.DeviceIdType.MESH)

    sib = z * 2 + o
    is_in = c == 0
    weights = [pltpu.make_async_copy(a.at[0], b, wsem.at[i])
               for i, (a, b) in enumerate(((wg_h, wg), (wu_h, wu), (wd_h, wd)))]
    for w in weights:
        w.start()

    peers = [lax.rem(e + i, E) for i in range(1, E)]
    chips = [lax.rem(z + i, C) for i in range(1, C)]
    barrier = pltpu.get_barrier_semaphore()

    def hello(expert, tp):
        pl.semaphore_signal(barrier, inc=1, device_id={"expert": expert, "tp": tp},
                            device_id_type=pl.DeviceIdType.MESH)
    hello(e, sib)
    for q in peers:
        hello(q, t)
    for q in chips:
        hello(e, q * 2 + c)
    pl.semaphore_wait(barrier, 1 + (E - 1) + (C - 1))

    swap[...] = jnp.where(is_in, grad[...].astype(F32), tok[...].astype(F32)).astype(BF16)
    gath[z, c] = jnp.where(is_in, tok[...].astype(F32), grad[...].astype(F32)).astype(BF16)
    metab[z, c] = jnp.zeros((8, 128), F32)
    for i, source in enumerate((ids, comb)):
        values = source[...].astype(F32)
        none = jnp.zeros_like(values)
        metab[z, c, 2 * i:2 * i + 2, :2 * n_tok] = jnp.concatenate(
            [jnp.where(is_in, values, none), jnp.where(is_in, none, values)], axis=1)

    near = jnp.minimum(z, C - 1 - z)

    def position(origin):
        far = jnp.abs(origin - z)
        return jnp.where(far <= near, jnp.where(origin < z, 2 * far - 1, 2 * far), near + far)
    a = remote(swap, gath.at[z, c], sw_s.at[0], sw_r.at[0], e, sib)
    b = remote(metab.at[z, c], metab.at[z, c], sw_s.at[1], sw_r.at[1], e, sib)
    a.start()
    b.start()
    a.wait_recv()
    b.wait_recv()

    def hop(origin, way):
        tp = (z + (1 if way == 0 else -1)) * 2 + c
        return (remote(gath.at[origin], gath.at[origin], ga_s.at[origin, way], ga_r.at[origin], e, tp),
                remote(metab.at[origin], metab.at[origin], me_s.at[origin, way], me_r.at[origin], e, tp))

    def send_on(origin, way):
        for d in hop(origin, way):
            d.start()

    can = (z + 1 < C, z >= 1)
    for way in (0, 1):
        pl.when(can[way])(functools.partial(send_on, z, way))

    def rows_out(origin, i, m):
        return remote(sendb.at[origin, peers[i]], X.at[c, m, e],
                      ex_s.at[origin, i], ex_r.at[m, i], peers[i], t)

    def process(origin):
        info = metab[origin, 0] + metab[origin, 1]
        sel, weight = routing(info, E, E * n_tok, 2 * n_tok)
        sel = sel.astype(BF16)
        picks[origin] = sel
        scale = jnp.where(is_in, jnp.ones_like(weight), weight)
        rows = dot(sel, gath[origin].reshape(2 * n_tok, D), 1, 0)
        sendb[origin] = (rows * scale).astype(BF16).reshape(E, n_tok, D)
        for i in range(E - 1):
            rows_out(origin, i, position(origin)).start()
        X[c, position(origin), e] = sendb[origin, e]

    def sibling_rows(kind, m):
        return remote(X.at[kind, m], X.at[kind, m], sx_s.at[m], sx_r.at[m], e, sib)

    def arrived(m):
        for i in range(E - 1):
            rows_out(0, i, m).wait_recv()
        sibling_rows(c, m).start()

    def take(origin, way):
        for d in hop(origin, way):
            d.wait_recv()
        pl.when(can[way])(functools.partial(send_on, origin, way))
        process(origin)

    process(z)
    for k in range(1, C):
        pl.when(z - k >= 0)(functools.partial(take, z - k, 0))
        pl.when(z + k < C)(functools.partial(take, z + k, 1))
    step = min(256, F)
    part_rows = C // 2
    half_rows = R // 2

    def hidden_units(h):
        for m in range(h * part_rows, (h + 1) * part_rows):
            sibling_rows(o, m).wait_recv()
        rows = pl.ds(h * half_rows, half_rows)

        @pl.loop(0, F // step)
        def _(n):
            cols = pl.ds(pl.multiple_of(n * step, step), step)
            rin = X[0, pl.ds(h * part_rows, part_rows)].reshape(half_rows, D)
            rgr = X[1, pl.ds(h * part_rows, part_rows)].reshape(half_rows, D)
            gate = dot(rin, wg[:, cols], 1, 0)
            up = dot(rin, wu[:, cols], 1, 0)
            gh = dot(rgr, wd[cols, :], 1, 1)
            s = jax.nn.sigmoid(gate)
            act = gate * s
            hid[rows, cols] = (act * up).astype(BF16)
            ggp[rows, cols] = (gh * up * s * (1.0 + gate * (1.0 - s))).astype(BF16)
            gup[rows, cols] = (gh * act).astype(BF16)

    for m in range(part_rows):
        arrived(m)
    for w in weights:
        w.wait()
    hidden_units(0)
    for m in range(part_rows, C):
        arrived(m)
    hidden_units(1)

    saves = [pltpu.make_async_copy(a, b, osem.at[i])
             for i, (a, b) in enumerate(((X.at[1], rgr_o), (ggp, ggp_o), (gup, gup_o)))]
    for s in saves:
        s.start()

    def back(half, n):
        at = pl.ds(pl.multiple_of(half * W + n * cw, cw), cw)
        return dot(ggp[...], wg[at, :], 1, 1) + dot(gup[...], wu[at, :], 1, 1)

    def sib_sum(n):
        return remote(sibs.at[n], sibr.at[n], si_s.at[n], si_r.at[n], e, sib)

    def part_out(n, i):
        return remote(part.at[n, :, peers[i]], ret.at[n, e], pa_s.at[n, i], pa_r.at[n, i], peers[i], t)

    def tok_out(n, i):
        return remote(tokp.at[n, chips[i]], zr.at[n, z], to_s.at[n, i], to_r.at[n, i], e, chips[i] * 2 + c)

    def fin_out(n):
        return remote(fin.at[n, o], got.at[n], fi_s.at[n], fi_r.at[n], e, sib)

    for n in range(PIECES):
        sibs[n] = back(o, n).astype(BF16)
        sib_sum(n).start()
    for n in range(PIECES):
        own = back(c, n)
        sib_sum(n).wait_recv()
        part[n] = (own + sibr[n].astype(F32)).astype(BF16).reshape(C, E, n_tok, cw)
        for i in range(E - 1):
            part_out(n, i).start()
        ret[n, e] = part[n, :, e]

    @pl.loop(0, D // 256)
    def _(n):
        at = pl.ds(pl.multiple_of(n * 256, 256), 256)
        rin_t[at, :] = X[0, :, :, :, at].reshape(R, 256).T

    @pl.loop(0, F // 256)
    def _(n):
        at = pl.ds(pl.multiple_of(n * 256, 256), 256)
        hid_t[at, :] = hid[:, at].T

    turned = [pltpu.make_async_copy(a, b, osem.at[3 + i])
              for i, (a, b) in enumerate(((rin_t, rin_o), (hid_t, hid_o)))]
    for s in turned:
        s.start()
    saves += turned

    def to_tokens(n, q):
        return dot(picks[q], ret[n, :, position(q)].reshape(E * n_tok, cw), 0, 0)

    for n in range(PIECES):
        for i in range(E - 1):
            part_out(n, i).wait_recv()
        for i in range(C - 1):
            tokp[n, chips[i]] = to_tokens(n, chips[i]).astype(BF16).reshape(2, n_tok, cw)
            tok_out(n, i).start()
    for n in range(PIECES):
        total = to_tokens(n, z)
        for i in range(C - 1):
            tok_out(n, i).wait_recv()
        for i in range(C - 1):
            total = total + zr[n, chips[i]].astype(F32).reshape(2 * n_tok, cw)
        fin[n] = total.astype(BF16).reshape(2, n_tok, cw)
        fin_out(n).start()
        gi_o[:, pl.ds(pl.multiple_of(c * W + n * cw, cw), cw)] = fin[n, c]
    for n in range(PIECES):
        fin_out(n).wait_recv()
        gi_o[:, pl.ds(pl.multiple_of(o * W + n * cw, cw), cw)] = got[n]

    a.wait_send()
    b.wait_send()

    def sent(origin, way):
        for d in hop(origin, way):
            d.wait_send()

    for way in (0, 1):
        pl.when(can[way])(functools.partial(sent, z, way))
    for k in range(1, C):
        pl.when(jnp.logical_and(z - k >= 0, can[0]))(functools.partial(sent, z - k, 0))
        pl.when(jnp.logical_and(z + k < C, can[1]))(functools.partial(sent, z + k, 1))
    for q in range(C):
        for i in range(E - 1):
            rows_out(q, i, q).wait_send()
        sibling_rows(c, q).wait_send()
    for n in range(PIECES):
        sib_sum(n).wait_send()
        for i in range(E - 1):
            part_out(n, i).wait_send()
        for i in range(C - 1):
            tok_out(n, i).wait_send()
        fin_out(n).wait_send()
    for s in saves:
        s.wait()


def weight_grads(rin, rgr, hid, ggp, gup, gg, gu, gd):
    x = rin[...]
    gg[0] = dot(x, ggp[...], 1, 0).astype(BF16)
    gu[0] = dot(x, gup[...], 1, 0).astype(BF16)
    gd[0] = dot(hid[...], rgr[...], 1, 0).astype(BF16)


def per_device(E, T, tokens_in, grad_out, expert_ids, combine, w_gate, w_up, w_down):
    n_tok, D = tokens_in.shape
    F = w_gate.shape[2]
    C = T // 2
    R = C * E * n_tok
    cw = D // 2 // PIECES
    any_, vm = pl.BlockSpec(memory_space=pl.ANY), pl.BlockSpec(memory_space=pltpu.VMEM)
    rows_t = jax.ShapeDtypeStruct((C, E, n_tok, D), BF16)
    ff_t = jax.ShapeDtypeStruct((R, F), BF16)
    V, S = pltpu.VMEM, pltpu.SemaphoreType.DMA
    rin, rgr, hid, ggp, gup, grad_input = pl.pallas_call(
        functools.partial(exchange, E, C),
        out_shape=(jax.ShapeDtypeStruct((D, R), BF16), rows_t, jax.ShapeDtypeStruct((F, R), BF16), ff_t, ff_t, jax.ShapeDtypeStruct((n_tok, D), BF16)),
        in_specs=[vm, vm, vm, vm, any_, any_, any_],
        out_specs=(any_, any_, any_, any_, any_, vm),
        scratch_shapes=[
            V((D, F), BF16), V((D, F), BF16), V((F, D), BF16),
            V((n_tok, D), BF16), V((C, 2, n_tok, D), BF16), V((C, 2, 8, 128), F32),
            V((C, E, n_tok, D), BF16), V((2, C, E, n_tok, D), BF16),
            V((C, E * n_tok, 2 * n_tok), BF16),
            V((R, F), BF16), V((R, F), BF16), V((R, F), BF16), V((D, R), BF16), V((F, R), BF16),
            V((PIECES, R, cw), BF16), V((PIECES, R, cw), BF16),
            V((PIECES, C, E, n_tok, cw), BF16), V((PIECES, E, C, n_tok, cw), BF16),
            V((PIECES, C, 2, n_tok, cw), BF16), V((PIECES, C, 2, n_tok, cw), BF16),
            V((PIECES, 2, n_tok, cw), BF16), V((PIECES, n_tok, cw), BF16),
            S((3,)), S((5,)), S((2,)), S((2,)),
            S((C, 2)), S((C,)), S((C, 2)), S((C,)),
            S((C, E - 1)), S((C, E - 1)), S((C,)), S((C,)),
            S((PIECES,)), S((PIECES,)), S((PIECES, E - 1)), S((PIECES, E - 1)),
            S((PIECES, C - 1)), S((PIECES, C - 1)), S((PIECES,)), S((PIECES,)),
        ],
        compiler_params=pltpu.CompilerParams(
            collective_id=0, has_side_effects=True, vmem_limit_bytes=VMEM_BYTES),
        cost_estimate=pl.CostEstimate(
            flops=10 * R * D * F, bytes_accessed=6 * D * F, transcendentals=R * F),
        name="exchange",
    )(tokens_in, grad_out, expert_ids.T, combine.T, w_gate, w_up, w_down)
    block = 1024
    whole = pl.BlockSpec((R, F), lambda i: (0, 0))
    cols = pl.BlockSpec((R, block), lambda i: (0, i))
    gg, gu, gd = pl.pallas_call(
        weight_grads,
        grid=(D // block,),
        out_shape=(jax.ShapeDtypeStruct((1, D, F), BF16), jax.ShapeDtypeStruct((1, D, F), BF16),
                   jax.ShapeDtypeStruct((1, F, D), BF16)),
        in_specs=[pl.BlockSpec((block, R), lambda i: (i, 0)), cols,
                  pl.BlockSpec((F, R), lambda i: (0, 0)), whole, whole],
        out_specs=(pl.BlockSpec((1, block, F), lambda i: (0, i, 0)),
                   pl.BlockSpec((1, block, F), lambda i: (0, i, 0)),
                   pl.BlockSpec((1, F, block), lambda i: (0, 0, i))),
        compiler_params=pltpu.CompilerParams(vmem_limit_bytes=VMEM_BYTES),
        cost_estimate=pl.CostEstimate(
            flops=6 * R * D * F, bytes_accessed=6 * D * F, transcendentals=0),
        name="weight_grads",
    )(rin, rgr.reshape(R, D), hid, ggp, gup)
    return grad_input, gg, gu, gd


def solution(mesh):
    rows = P(("expert", "tp"), None)
    columns = P("expert", None, "tp")
    return jax.shard_map(
        functools.partial(per_device, mesh.shape["expert"], mesh.shape["tp"]),
        mesh=mesh,
        in_specs=(rows, rows, rows, rows, columns, columns, P("expert", "tp", None)),
        out_specs=(rows, columns, columns, P("expert", "tp", None)),
        check_vma=False,
    )
```
